128 devices in a mesh: inst: 16 (over z_hi, y, core), blk: 8 (over x, z_lo).
Axes of the slice: x: 4, y: 4, z: 4 (z_hi: 2, z_lo: 2; z = z_hi * 2 + z_lo), core: 2. Of those that a mesh axis runs over, the one named last changes fastest.
Arguments:
- queries: bfloat16 [16384, 8192], P(('inst', 'blk')), may hold values from -16 to 16
- keys: bfloat16 [16384, 1024], P(('inst', 'blk')), may hold values from -16 to 16
- values: bfloat16 [16384, 1024], P(('inst', 'blk')), may hold values from -6 to 6
- lengths: int32 [8], replicated, may hold values from 1 to 4, as said below
Outputs:
- attended: bfloat16 [16384, 8192], P(('inst', 'blk'))
The draws below stay inside these ranges and needn't reach their ends.
Inputs may be any that keep to these rules, and one draw needn't show every extreme that they name: The lengths sum to 16; one request covers exactly 4 instances.
All inputs are finite; a program needn't handle non-finite values.
Results may differ from the reference program's by a relative error of at most 0.0085.
Values may be sent and summed in bfloat16 or wider, within the bound.
A program may use at most 320 MiB of HBM per device.

```python
import jax
import jax.numpy as jnp
from jax import lax

QUERY_HEADS = 64
KEY_VALUE_HEADS = 8
HEAD_SIZE = 128
TQ = 128
MAXSPAN = 4
QUERY_PER_KEY = 8
REQUESTS = 8
TOKEN_TOTAL = 16384
N_INST = 16
N_BLK = 8


def draw_lengths(key, part):
    key = jax.random.fold_in(key, 13)
    spread_key, place_key = jax.random.split(key)
    others = REQUESTS - 1
    surplus = 2 * REQUESTS - MAXSPAN - others
    slot_owner = jnp.repeat(jnp.arange(others, dtype=jnp.int32), MAXSPAN - 1)
    shuffled = jax.random.permutation(spread_key, slot_owner)
    chosen = shuffled[:surplus]
    extra_count = jnp.sum((chosen[:, None] == jnp.arange(others, dtype=jnp.int32)[None, :]).astype(jnp.int32), axis=0)
    rest = 1 + extra_count
    joined = jnp.concatenate([jnp.full((1,), MAXSPAN, jnp.int32), rest.astype(jnp.int32)])
    offset = jax.random.randint(place_key, (), 0, REQUESTS)
    return jnp.roll(joined, offset).astype(jnp.int32)


def draw_keys(key, part):
    key = jax.random.fold_in(key, 11)
    leading_key = jax.random.fold_in(key, 0)
    base_offset = jnp.clip(jax.random.normal(leading_key, (TOKEN_TOTAL, KEY_VALUE_HEADS, HEAD_SIZE), jnp.float32), -6.0, 6.0)
    return base_offset.reshape(TOKEN_TOTAL, KEY_VALUE_HEADS * HEAD_SIZE).astype(jnp.bfloat16)


def draw_queries(key, part):
    key = jax.random.fold_in(key, 12)
    leading_key = jax.random.fold_in(key, 0)
    base_offset = jnp.clip(jax.random.normal(leading_key, (TOKEN_TOTAL, QUERY_HEADS, HEAD_SIZE), jnp.float32), -6.0, 6.0)
    return base_offset.reshape(TOKEN_TOTAL, QUERY_HEADS * HEAD_SIZE).astype(jnp.bfloat16)


def block_scale(rng, shape, pieces, least, largest):
    gain, own = 1.0, jax.random.fold_in(rng, 6)
    for position, parts in pieces:
        draws = jnp.exp(jax.random.uniform(jax.random.fold_in(own, position), (parts,), jnp.float32, least / len(pieces), largest / len(pieces)))
        gain = gain * jnp.repeat(draws, shape[position] // parts).reshape([-1 if axis == position else 1 for axis in range(len(shape))])
    return gain


def gaussian(key, extent, scale, bound, pieces=(), kind=jnp.bfloat16):
    loudness = block_scale(key, extent, pieces, -0.22, 0.18) if pieces else 1.0
    values = jax.random.normal(key, extent, jnp.float32) * scale * loudness
    return jnp.minimum(jnp.maximum(values, -bound), bound).astype(kind)


def setup_inputs(seed: int = 0) -> dict:
    seeds = jax.random.split(jax.random.key(seed), 5)
    return {
        "queries": draw_queries(jax.random.fold_in(seeds[4], 71), 0),
        "keys": draw_keys(jax.random.fold_in(seeds[4], 71), 0),
        "values": gaussian(seeds[2], (TOKEN_TOTAL, KEY_VALUE_HEADS * HEAD_SIZE), 1.0, 6.0, ((0, 128),)),
        "lengths": draw_lengths(jax.random.fold_in(seeds[4], 71), 0),
    }


def reference(queries, keys, values, lengths):
    stretch_factor = TQ * N_BLK
    request_span = MAXSPAN * stretch_factor
    scale = HEAD_SIZE ** -0.5
    ends = jnp.cumsum(lengths)

    def one_instance(inst_id):
        start_inst = jnp.max(jnp.where(ends <= inst_id, ends, 0))
        lowest = start_inst * stretch_factor
        first = jnp.maximum(inst_id - (MAXSPAN - 1), 0)
        query_rows = lax.dynamic_slice_in_dim(queries, (inst_id * stretch_factor).astype(jnp.int32), stretch_factor, 0)
        key_rows = lax.dynamic_slice_in_dim(keys, (first * stretch_factor).astype(jnp.int32), request_span, 0)
        value_rows = lax.dynamic_slice_in_dim(values, (first * stretch_factor).astype(jnp.int32), request_span, 0)
        qpos = inst_id * stretch_factor + jnp.arange(stretch_factor, dtype=jnp.int32)
        kpos = first * stretch_factor + jnp.arange(request_span, dtype=jnp.int32)
        allowed = (kpos[None, :] >= lowest) & (kpos[None, :] <= qpos[:, None])
        query_heads = query_rows.reshape(stretch_factor, KEY_VALUE_HEADS, QUERY_PER_KEY, HEAD_SIZE).transpose(1, 0, 2, 3)
        key_heads = key_rows.reshape(request_span, KEY_VALUE_HEADS, HEAD_SIZE).transpose(1, 0, 2)
        value_heads = value_rows.reshape(request_span, KEY_VALUE_HEADS, HEAD_SIZE).transpose(1, 0, 2)

        def one_head(item):
            q_one, k_one, v_one = item
            scores = jnp.einsum("cgd,kd->cgk", q_one.astype(jnp.float32), k_one.astype(jnp.float32)) * scale
            mask = allowed[:, None, :]
            scores = jnp.where(mask, scores, -1e30)
            top = jnp.max(scores, axis=-1, keepdims=True)
            weights = jnp.where(mask, jnp.exp(scores - top), 0.0)
            grand_total = jnp.sum(weights, axis=-1, keepdims=True)
            rounded = weights.astype(jnp.bfloat16).astype(jnp.float32)
            summed_output = jnp.einsum("cgk,kd->cgd", rounded, v_one.astype(jnp.float32))
            return summed_output / grand_total

        heads_out = lax.map(one_head, (query_heads, key_heads, value_heads))
        return heads_out.transpose(1, 0, 2, 3).reshape(stretch_factor, QUERY_HEADS * HEAD_SIZE).astype(jnp.bfloat16)

    blocks = lax.map(one_instance, jnp.arange(N_INST, dtype=jnp.int32))
    return blocks.reshape(TOKEN_TOTAL, QUERY_HEADS * HEAD_SIZE)
```

```python
import itertools
import math

import jax
import jax.numpy as jnp
from jax import lax
from jax.experimental import pallas as pl
from jax.experimental.pallas import tpu as pltpu
from jax.sharding import PartitionSpec as P

MESH = pl.DeviceIdType.MESH
HEAD = 128
TOK = 128
GROUPS = 4
HB = 4
ROWS = HB * TOK
HALF = GROUPS * HEAD
SCALE = HEAD**-0.5 * math.log2(math.e)
FAR = 1e30

JOBS = (
    ((0, True, "x"), (1, True, "x"),),
    ((0, True, "xl"), (1, True, "xl"), (0, True, "xr"), (1, True, "xr"), (0, False, "x"), (1, False, "x"),),
    ((2, True, "x"), (3, True, "x"), (2, False, "x"), (3, False, "x"),),
    ((0, False, "xl"), (0, False, "xr"), (0, True, "xx"), (0, False, "xx"), (1, False, "xl"), (1, False, "xr"), (1, True, "xx"), (1, False, "xx"),),
    ((2, True, "xl"), (2, True, "xr"), (3, True, "xl"), (3, True, "xr"),),
    ((4, True, "x"), (4, False, "x"), (4, True, "xl"), (4, True, "xr"),),
    ((2, False, "xl"), (2, False, "xr"), (3, False, "xl"), (3, False, "xr"),),
    ((4, True, "xx"), (4, False, "xx"), (4, False, "xl"), (4, False, "xr"),),
    ((2, True, "xx"), (2, False, "xx"), (3, True, "xx"), (3, False, "xx"),),
)
EVENTS = (
    (1, 0, False, "x", 0),
    (2, 0, False, "x", 1),
    (3, 2, True, "x", 0),
    (4, 1, True, "xl", 0),
    (4, 0, True, "xr", 0),
    (4, 1, True, "xr", 0),
    (4, 1, False, "x", 0),
    (4, 0, True, "xl", 0),
    (5, 0, True, "xl", 1),
    (5, 2, True, "x", 1),
    (6, 3, True, "x", 0),
    (6, 1, True, "xl", 1),
    (6, 1, True, "xr", 1),
    (6, 0, True, "xr", 1),
    (6, 1, False, "x", 1),
    (7, 3, True, "x", 1),
    (7, 0, False, "xl", 1),
    (7, 0, False, "xr", 1),
    (7, 0, False, "xr", 0),
    (7, 0, False, "xl", 0),
    (7, 2, False, "x", 0),
    (8, 2, False, "x", 1),
    (8, 3, True, "xl", 0),
    (8, 1, False, "xl", 0),
    (8, 1, True, "xx", 0),
    (8, 3, False, "x", 0),
    (9, 2, True, "xr", 0),
    (10, 1, False, "xr", 0),
    (10, 3, False, "x", 1),
    (10, 0, True, "xx", 0),
    (11, 1, True, "xx", 1),
    (11, 0, True, "xx", 1),
    (11, 1, False, "xx", 0),
    (12, 3, True, "xr", 0),
    (12, 2, True, "xl", 0),
    (12, 1, False, "xr", 1),
    (12, 0, False, "xx", 0),
    (13, 1, False, "xl", 1),
    (14, 2, False, "xl", 0),
    (14, 4, True, "x", 0),
    (14, 1, False, "xx", 1),
    (14, 2, True, "xl", 1),
    (14, 0, False, "xx", 1),
    (16, 3, True, "xl", 1),
    (16, 4, False, "x", 0),
    (18, 2, True, "xr", 1),
    (18, 2, False, "xr", 0),
    (18, 3, True, "xr", 1),
    (19, 4, True, "x", 1),
    (20, 4, True, "xl", 0),
    (20, 4, True, "xr", 0),
    (21, 3, True, "xx", 0),
    (22, 3, False, "xr", 1),
    (22, 3, False, "xr", 0),
    (22, 4, True, "xl", 1),
    (22, 4, True, "xr", 1),
    (22, 3, False, "xl", 0),
    (22, 4, False, "x", 1),
    (22, 3, False, "xl", 1),
    (23, 2, False, "xl", 1),
    (23, 2, True, "xx", 0),
    (24, 4, False, "xr", 0),
    (24, 4, True, "xx", 0),
    (25, 4, False, "xr", 1),
    (26, 4, True, "xx", 1),
    (26, 2, False, "xr", 1),
    (27, 4, False, "xl", 1),
    (28, 4, False, "xx", 0),
    (28, 3, True, "xx", 1),
    (28, 2, True, "xx", 1),
    (28, 4, False, "xl", 0),
    (30, 4, False, "xx", 1),
    (31, 3, False, "xx", 0),
    (32, 2, False, "xx", 0),
    (32, 3, False, "xx", 1),
    (34, 2, False, "xx", 1),
)
RELAY = (
    (0, 2, "x", 0),
    (3, 2, "x", 1),
    (4, 3, "x", 0),
    (5, 3, "x", 1),
    (6, 3, "xl", 0),
    (6, 2, "xr", 0),
    (7, 3, "xr", 0),
    (8, 2, "xl", 0),
    (9, 2, "xl", 1),
    (10, 4, "x", 0),
    (12, 3, "xl", 1),
    (12, 3, "xr", 1),
    (13, 2, "xr", 1),
    (14, 4, "x", 1),
    (14, 3, "xx", 0),
    (15, 2, "xx", 0),
    (15, 3, "xx", 1),
    (15, 2, "xx", 1),
)


def kernel(len_ref, q_ref, k_ref, v_ref, o_ref, kv, stage_s, kin, vin, qbuf, obuf, acc_s, m_s, l_s, bias_s,
           rs, ss, loc, core_send, core_recv, osem):
    inst, b = lax.axis_index("inst"), lax.axis_index("blk")
    c, row = lax.rem(inst, 2), inst // 2
    other = 1 - c
    z, x = lax.rem(b, 2), b // 2
    zo = 1 - z
    xr, xl, xx = lax.rem(x + 1, 4), lax.rem(x + 3, 4), lax.rem(x + 2, 4)
    dev_xr, dev_xl = (inst, xr * 2 + z), (inst, xl * 2 + z)
    dev_z = (inst, x * 2 + zo)
    dev_core = (inst + 1 - 2 * c, b)
    y, zh = lax.rem(row, 4), row // 4
    dev_up = ((zh * 4 + lax.rem(y + 1, 4)) * 2 + c, b)
    dev_down = ((zh * 4 + lax.rem(y + 3, 4)) * 2 + c, b)
    dev_outer = ((4 - row) * 2 + c, x * 2 + zo)
    at_end = jnp.logical_or(row == 0, row == 4)
    z1 = jnp.where(row == 4, zo, z)
    z2 = jnp.where(jnp.logical_or(row == 4, row == 5), zo, z)

    q_cols = lambda half: pl.ds(pl.multiple_of(half * (8 * HALF), HEAD), 8 * HALF)
    locals_ = [
        pltpu.make_async_copy(k_ref, kin, loc.at[0]),
        pltpu.make_async_copy(v_ref, vin, loc.at[1]),
        pltpu.make_async_copy(q_ref.at[:, q_cols(c)], qbuf.at[c], loc.at[2]),
    ]
    for copy in locals_:
        copy.start()

    barrier = pltpu.get_barrier_semaphore()
    for dev in (dev_xr, dev_xl, dev_z, dev_core, dev_up, dev_down):
        pl.semaphore_signal(barrier, inc=1, device_id=dev, device_id_type=MESH)

    @pl.when(at_end)
    def _():
        pl.semaphore_signal(barrier, inc=1, device_id=dev_outer, device_id_type=MESH)

    pl.semaphore_wait(barrier, jnp.where(at_end, 7, 6))

    def core_copy(src, dst, n):
        return pltpu.make_async_remote_copy(
            src_ref=src, dst_ref=dst, send_sem=core_send.at[n], recv_sem=core_recv.at[n],
            device_id=dev_core, device_id_type=MESH)

    cores = [
        core_copy(q_ref.at[:, q_cols(other)], qbuf.at[c], 0),
        core_copy(stage_s, kv.at[c, z, x], 1),
    ]
    cores[0].start()

    sends = []

    def send(src, dst, dev, cond=None, inside=None):
        place = len(sends)

        def copy():
            return pltpu.make_async_remote_copy(
                src_ref=kv.at[src], dst_ref=kv.at[dst], send_sem=ss.at[place],
                recv_sem=rs.at[dst], device_id=dev, device_id_type=MESH)

        sends.append((copy, [one for one in (cond, inside) if one is not None]))
        if cond is None:
            copy().start()
        else:
            pl.when(cond)(lambda: copy().start())

    def arrived(slot):
        pltpu.make_async_remote_copy(
            src_ref=kv.at[slot], dst_ref=kv.at[slot], send_sem=ss.at[0],
            recv_sem=rs.at[slot], device_id=dev_xr, device_id_type=MESH).wait_recv()

    first_row, not_first, not_last = row == 0, row != 0, row != 7

    def up(src, kind, inside=None):
        send(src, (kind,) + src[1:], dev_up, not_last, inside)

    def own(t):
        for half in range(2):
            slot = (t, z, x, half)
            for dev in (dev_xr, dev_xl, dev_z):
                send(slot, slot, dev)
            up(slot, t + 2)

    def fill(dst, half):
        for g in range(GROUPS):
            cols = pl.ds(pl.multiple_of((half * GROUPS + g) * HEAD, HEAD), HEAD)
            dst[g // 2, 0, g % 2] = kin[:, cols].astype(jnp.float32).T.astype(jnp.bfloat16)
            dst[g // 2, 1, g % 2] = vin[:, cols]

    for copy in locals_[:2]:
        copy.wait()
    fill(stage_s, other)
    cores[1].start()
    fill(kv.at[c, z, x], c)
    own(c)
    cores[1].wait_recv()
    own(other)

    tt = lax.broadcasted_iota(jnp.int32, (TOK, TOK), 0)
    kk = lax.broadcasted_iota(jnp.int32, (TOK, TOK), 1)
    bias_s[...] = jnp.where(kk <= tt, 0.0, -FAR)

    def start_of(i):
        total, first = len_ref[0] * 0, len_ref[0] * 0
        for r in range(8):
            total = total + len_ref[r]
            first = jnp.where(total <= i, total, first)
        return first

    start0, start1 = start_of(2 * row), start_of(2 * row + 1)

    def fine(start, key_inst):
        return jnp.where(start <= key_inst, 0.0, FAR).astype(jnp.float32)

    z1o, z2o = 1 - z1, 1 - z2
    places = {"x": x, "xl": xl, "xr": xr, "xx": xx}

    def slot_of(t, near, place):
        home, away = (z, zo) if t < 2 else (z1, z1o) if t < 4 else (z2, z2o)
        return (t, home if near else away, places[place])

    def event(t, near, place, half):
        slot = slot_of(t, near, place) + (half,)
        inside = None if t < 2 else not_first
        on = lambda *devs: [send(slot, slot, dev, None, inside) for dev in devs]
        arrived(slot)
        if not near:
            if place == "x":
                on(dev_xr, dev_xl)
        elif t < 2:
            if place == "xx":
                on(dev_z)
            elif (t, place) == (0, "xl"):
                on(dev_xr)
            elif (t, place) == (1, "xr"):
                on(dev_xl)
            up(slot, t + 2)
        elif t < 4:
            if place in ("x", "xx"):
                on(dev_z)
            if (t, place) == (3, "x"):
                up(slot, 4, not_first)
        elif place == "x":
            on(dev_xr, dev_xl, dev_z)
        elif place == "xl":
            on(dev_xr)
        elif place == "xx":
            on(dev_z)

    def relay(piece):
        for at, t, place, half in RELAY:
            if at != piece:
                continue
            slot = (t, z, places[place], half)
            arrived(slot)
            send(slot, slot, dev_outer, None, first_row)
            if (t, place) == (3, "x"):
                up(slot, 4, first_row)

    def events_at(piece):
        if any(one[0] == piece for one in RELAY):
            pl.when(first_row)(lambda: relay(piece))
        here = [one[1:] for one in EVENTS if one[0] == piece]
        for common, run_ in itertools.groupby(here, key=lambda one: one[0] < 2):
            several = list(run_)

            def go():
                for one in several:
                    event(*one)

            if common:
                go()
            else:
                pl.when(not_first)(go)

    own_even = fine(start1, 2 * row)
    flags = {(qp, t): fine((start0, start1)[qp], 2 * row + back)
             for qp in range(2) for t, back in ((2, -2), (3, -1), (4, -3))}
    earlier = {
        (near, place): jnp.where(places[place] * 2 + (z if near else zo) < b, 0.0, -FAR).astype(jnp.float32)
        for near in (True, False) for place in places}

    def tiles_of(job, qp):
        tiles = []
        for t, near, place in job:
            slot = slot_of(t, near, place)
            if t == 0 and qp == 1:
                tiles.append((slot, own_even, None))
            elif t == qp:
                tiles.append((slot, None, "own" if near and place == "x" else earlier[near, place]))
            elif t in (2, 3) or (t == 4 and qp == 0):
                tiles.append((slot, flags[qp, t], None))
        return tiles

    def run(number, job, everywhere=False, final=False):
        first = number == 0
        units = [(hb, qp, tiles_of(job, qp)) for qp in range(2) for hb in range(8 // HB)]
        units = [unit for unit in units if unit[2]]

        def compute(g):
            def head_cols(hb, h):
                return pl.ds(pl.multiple_of((g * 8 + hb * HB + h) * HEAD, HEAD), HEAD)

            def scores(unit):
                hb, qp, tiles = unit
                q = jnp.concatenate([qbuf[qp, :, head_cols(hb, h)] for h in range(HB)], axis=0)
                k = jnp.concatenate([kv[slot + (lax.div(g, 2), 0, lax.rem(g, 2))] for slot, _, _ in tiles], axis=1)
                got = jnp.dot(q, k, preferred_element_type=jnp.float32)
                out = []
                for n, (_, _, add) in enumerate(tiles):
                    sc = got[:, n * HEAD:(n + 1) * HEAD]
                    if isinstance(add, str):
                        sc = (sc.reshape(HB, TOK, TOK) + bias_s[...][None]).reshape(ROWS, TOK)
                    elif add is not None:
                        sc = sc + add
                    out.append(sc)
                return out

            def fold(unit, scs):
                hb, qp, tiles = unit
                span = pl.ds(hb * ROWS, ROWS)
                state = g * 2 + qp
                groups = {}
                for sc, (_, pen, _) in zip(scs, tiles):
                    groups.setdefault(id(pen), (pen, []))[1].append(sc)
                best = None
                for pen, members in groups.values():
                    top = members[0]
                    for one in members[1:]:
                        top = jnp.maximum(top, one)
                    top = jnp.max(top, axis=-1, keepdims=True) * SCALE
                    top = top if pen is None else top - pen
                    best = top if best is None else jnp.maximum(best, top)
                best = jnp.broadcast_to(best, (ROWS, HEAD))
                if not first:
                    old = m_s[state, span, :]
                    best = jnp.maximum(old, best)
                    factor = jnp.exp2(old - best)
                shifts = {key: best if pen is None else best + pen for key, (pen, _) in groups.items()}
                ws = [jnp.exp2(sc * SCALE - shifts[id(pen)]) for sc, (_, pen, _) in zip(scs, tiles)]
                total = ws[0]
                for one in ws[1:]:
                    total = total + one
                w = jnp.concatenate([one.astype(jnp.bfloat16) for one in ws], axis=1)
                v = jnp.concatenate([kv[slot + (lax.div(g, 2), 1, lax.rem(g, 2))] for slot, _, _ in tiles], axis=0)
                part = jnp.dot(w, v, preferred_element_type=jnp.float32)
                if not first:
                    total = l_s[state, span, :] * factor + total
                    part = acc_s[state, span, :] * factor + part
                if final:
                    res = (part / jnp.sum(total, axis=-1, keepdims=True)).astype(jnp.bfloat16)
                    for h in range(HB):
                        obuf[qp, :, head_cols(hb, h)] = res[h * TOK:(h + 1) * TOK]
                else:
                    m_s[state, span, :] = best
                    l_s[state, span, :] = total
                    acc_s[state, span, :] = part

            ahead = scores(units[0])
            for n, unit in enumerate(units):
                scs = ahead
                if n + 1 < len(units):
                    ahead = scores(units[n + 1])
                fold(unit, scs)
            if final:
                for copy in results(g):
                    copy.start()

        def body(g, carry):
            for at in range(1, GROUPS):
                if any(e[0] == number * GROUPS + at for e in EVENTS + RELAY):
                    pl.when(g == at)(lambda at=at: events_at(number * GROUPS + at))
            if everywhere:
                compute(g)
            else:
                pl.when(not_first)(lambda: compute(g))
            return carry

        events_at(number * GROUPS)
        lax.fori_loop(0, GROUPS, body, 0)

    def results(g):
        cols = pl.ds(pl.multiple_of(g * (8 * HEAD), HEAD), 8 * HEAD)
        ocols = pl.ds(pl.multiple_of((c * GROUPS + g) * (8 * HEAD), HEAD), 8 * HEAD)
        return (
            pltpu.make_async_copy(obuf.at[c, :, cols], o_ref.at[:, ocols], osem.at[0, g]),
            pltpu.make_async_remote_copy(
                src_ref=obuf.at[other, :, cols], dst_ref=o_ref.at[:, ocols],
                send_sem=osem.at[1, g], recv_sem=osem.at[2, g],
                device_id=dev_core, device_id_type=MESH),
        )

    locals_[2].wait()
    cores[0].wait_recv()
    shared = [job[0][0] < 2 for job in JOBS]
    last_shared = max(n for n, one in enumerate(shared) if one)
    for number in range(last_shared + 1):
        run(number, JOBS[number], everywhere=shared[number])

    @pl.when(first_row)
    def _():
        def body(g, carry):
            for qp in range(2):
                for h in range(8):
                    span = pl.ds(h * TOK, TOK)
                    total = jnp.sum(l_s[g * 2 + qp, span, :], axis=-1, keepdims=True)
                    cols = pl.ds(pl.multiple_of((g * 8 + h) * HEAD, HEAD), HEAD)
                    obuf[qp, :, cols] = (acc_s[g * 2 + qp, span, :] / total).astype(jnp.bfloat16)
            for copy in results(g):
                copy.start()
            return carry

        lax.fori_loop(0, GROUPS, body, 0)

    for number in range(last_shared + 1, len(JOBS)):
        run(number, JOBS[number], final=number == len(JOBS) - 1)

    assert len(sends) <= 112
    for copy, conds in sends:
        if conds:
            cond = conds[0] if len(conds) == 1 else jnp.logical_and(*conds)
            pl.when(cond)(lambda copy=copy: copy().wait_send())
        else:
            copy().wait_send()
    for copy in cores:
        copy.wait_send()
    for g in range(GROUPS):
        mine, theirs = results(g)
        mine.wait()
        theirs.wait()


def local(queries, keys, values, lengths):
    dma = pltpu.SemaphoreType.DMA
    anywhere = pl.BlockSpec(memory_space=pl.ANY)
    return pl.pallas_call(
        kernel,
        out_shape=jax.ShapeDtypeStruct(queries.shape, jnp.bfloat16),
        in_specs=[pl.BlockSpec(memory_space=pltpu.SMEM), anywhere, anywhere, anywhere],
        out_specs=anywhere,
        scratch_shapes=[
            pltpu.VMEM((5, 2, 4, 2, 2, 2, TOK, HEAD), jnp.bfloat16),
            pltpu.VMEM((2, 2, 2, TOK, HEAD), jnp.bfloat16),
            pltpu.VMEM((TOK, 2 * HALF), jnp.bfloat16),
            pltpu.VMEM((TOK, 2 * HALF), jnp.bfloat16),
            pltpu.VMEM((2, TOK, 8 * HALF), jnp.bfloat16),
            pltpu.VMEM((2, TOK, 8 * HALF), jnp.bfloat16),
            pltpu.VMEM((2 * GROUPS, 8 * TOK, HEAD), jnp.float32),
            pltpu.VMEM((2 * GROUPS, 8 * TOK, HEAD), jnp.float32),
            pltpu.VMEM((2 * GROUPS, 8 * TOK, HEAD), jnp.float32),
            pltpu.VMEM((TOK, TOK), jnp.float32),
            dma((5, 2, 4, 2)),
            dma((112,)),
            dma((3,)),
            dma((2,)),
            dma((2,)),
            dma((3, GROUPS)),
        ],
        compiler_params=pltpu.CompilerParams(
            collective_id=0, has_side_effects=True, vmem_limit_bytes=58 * 1024 * 1024),
        cost_estimate=pl.CostEstimate(flops=30_000_000_000, bytes_accessed=8_000_000, transcendentals=40_000_000),
    )(lengths, queries, keys, values)


def solution(mesh):
    split = P(("inst", "blk"), None)
    return jax.shard_map(local, mesh=mesh, in_specs=(split, split, split, P()), out_specs=split, check_vma=False)
```

```python
import itertools
import math

import jax
import jax.numpy as jnp
from jax import lax
from jax.experimental import pallas as pl
from jax.experimental.pallas import tpu as pltpu
from jax.sharding import PartitionSpec as P

MESH = pl.DeviceIdType.MESH
HEAD = 128
TOK = 128
GROUPS = 4
HB = 4
ROWS = HB * TOK
HALF = GROUPS * HEAD
SCALE = HEAD**-0.5 * math.log2(math.e)
FAR = 1e30

JOBS = (
    ((0, True, "x"), (1, True, "x"),),
    ((0, True, "xl"), (1, True, "xl"), (0, True, "xr"), (1, True, "xr"), (0, False, "x"), (1, False, "x"),),
    ((2, True, "x"), (3, True, "x"), (2, False, "x"), (3, False, "x"),),
    ((0, False, "xl"), (0, False, "xr"), (0, True, "xx"), (0, False, "xx"), (1, False, "xl"), (1, False, "xr"), (1, True, "xx"), (1, False, "xx"),),
    ((2, True, "xl"), (2, True, "xr"), (3, True, "xl"), (3, True, "xr"),),
    ((4, True, "x"), (4, False, "x"), (4, True, "xl"), (4, True, "xr"),),
    ((2, False, "xl"), (2, False, "xr"), (3, False, "xl"), (3, False, "xr"),),
    ((4, True, "xx"), (4, False, "xx"), (4, False, "xl"), (4, False, "xr"),),
    ((2, True, "xx"), (2, False, "xx"), (3, True, "xx"), (3, False, "xx"),),
)
EVENTS = (
    (0, 0, False, "x", 1),
    (0, 0, False, "x", 0),
    (1, 2, True, "x", 1),
    (1, 2, True, "x", 0),
    (1, 0, True, "xl", 0),
    (1, 1, False, "x", 0),
    (2, 3, True, "x", 0),
    (2, 0, True, "xr", 0),
    (2, 1, True, "xr", 0),
    (2, 1, False, "x", 1),
    (2, 1, True, "xl", 0),
    (3, 3, True, "x", 1),
    (3, 0, True, "xl", 1),
    (3, 1, True, "xr", 1),
    (3, 0, True, "xr", 1),
    (3, 1, True, "xl", 1),
    (4, 0, False, "xl", 0),
    (4, 4, True, "x", 0),
    (4, 1, True, "xx", 0),
    (4, 0, False, "xl", 1),
    (4, 0, True, "xx", 0),
    (4, 2, False, "x", 0),
    (4, 3, False, "x", 0),
    (5, 2, False, "x", 1),
    (5, 1, False, "xl", 1),
    (5, 3, False, "x", 1),
    (5, 1, False, "xr", 0),
    (6, 0, False, "xr", 1),
    (6, 1, True, "xx", 1),
    (6, 1, False, "xl", 0),
    (6, 1, False, "xr", 1),
    (6, 2, True, "xr", 0),
    (6, 0, True, "xx", 1),
    (6, 0, False, "xx", 0),
    (6, 4, True, "xl", 0),
    (6, 3, True, "xr", 0),
    (6, 1, False, "xx", 0),
    (6, 0, False, "xr", 0),
    (7, 2, False, "xr", 0),
    (7, 4, True, "x", 1),
    (7, 4, False, "x", 0),
    (7, 4, True, "xr", 0),
    (7, 2, False, "xl", 0),
    (7, 0, False, "xx", 1),
    (7, 1, False, "xx", 1),
    (8, 3, True, "xr", 1),
    (8, 3, False, "xl", 0),
    (8, 3, False, "xr", 0),
    (8, 2, False, "xr", 1),
    (8, 2, True, "xl", 0),
    (8, 3, True, "xl", 0),
    (9, 2, True, "xl", 1),
    (9, 3, False, "xl", 1),
    (9, 2, False, "xl", 1),
    (9, 3, False, "xr", 1),
    (9, 2, True, "xr", 1),
    (9, 3, True, "xl", 1),
    (9, 4, True, "xx", 0),
    (10, 3, True, "xx", 0),
    (10, 4, True, "xl", 1),
    (11, 4, True, "xr", 1),
    (11, 4, False, "x", 1),
    (12, 2, True, "xx", 0),
    (13, 4, True, "xx", 1),
    (13, 4, False, "xx", 0),
    (14, 2, True, "xx", 1),
    (14, 4, False, "xl", 0),
    (14, 4, False, "xr", 0),
    (15, 4, False, "xl", 1),
    (15, 3, True, "xx", 1),
    (15, 4, False, "xx", 1),
    (15, 4, False, "xr", 1),
    (16, 3, False, "xx", 0),
    (16, 2, False, "xx", 0),
    (17, 2, False, "xx", 1),
    (17, 3, False, "xx", 1),
)
RELAY = (
    (0, 2, "x", 0),
    (0, 2, "x", 1),
    (0, 3, "x", 0),
    (1, 3, "x", 1),
    (1, 2, "xl", 0),
    (1, 4, "x", 0),
    (1, 2, "xr", 0),
    (2, 3, "xr", 0),
    (3, 3, "xl", 0),
    (3, 4, "x", 1),
    (4, 2, "xl", 1),
    (5, 3, "xr", 1),
    (5, 2, "xr", 1),
    (6, 3, "xl", 1),
    (6, 3, "xx", 0),
    (7, 2, "xx", 0),
    (7, 3, "xx", 1),
    (7, 2, "xx", 1),
)


def kernel(len_hbm, q_ref, k_ref, v_ref, o_ref, kv, stage_s, kin, vin, qbuf, qs, obuf, acc_s, m_s, l_s, bias_s,
           len_ref, rs, ss, loc, core_send, core_recv, osem):
    inst, b = lax.axis_index("inst"), lax.axis_index("blk")
    c, row = lax.rem(inst, 2), inst // 2
    other = 1 - c
    z, x = lax.rem(b, 2), b // 2
    zo = 1 - z
    xr, xl, xx = lax.rem(x + 1, 4), lax.rem(x + 3, 4), lax.rem(x + 2, 4)
    dev_xr, dev_xl = (inst, xr * 2 + z), (inst, xl * 2 + z)
    dev_z = (inst, x * 2 + zo)
    dev_core = (inst + 1 - 2 * c, b)
    y, zh = lax.rem(row, 4), row // 4
    dev_up = ((zh * 4 + lax.rem(y + 1, 4)) * 2 + c, b)
    dev_down = ((zh * 4 + lax.rem(y + 3, 4)) * 2 + c, b)
    dev_outer = ((4 - row) * 2 + c, x * 2 + zo)
    at_end = jnp.logical_or(row == 0, row == 4)
    z1 = jnp.where(row == 4, zo, z)
    z2 = jnp.where(jnp.logical_or(row == 4, row == 5), zo, z)

    q_cols = lambda half: pl.ds(pl.multiple_of(half * (8 * HALF), HEAD), 8 * HALF)
    locals_ = [
        pltpu.make_async_copy(k_ref, kin, loc.at[0]),
        pltpu.make_async_copy(v_ref, vin, loc.at[1]),
        pltpu.make_async_copy(q_ref.at[:, q_cols(c)], qbuf.at[c], loc.at[2]),
        pltpu.make_async_copy(len_hbm, len_ref, loc.at[3]),
    ]
    for copy in locals_:
        copy.start()

    barrier = pltpu.get_barrier_semaphore()
    for dev in (dev_xr, dev_xl, dev_z, dev_core, dev_up, dev_down):
        pl.semaphore_signal(barrier, inc=1, device_id=dev, device_id_type=MESH)

    @pl.when(at_end)
    def _():
        pl.semaphore_signal(barrier, inc=1, device_id=dev_outer, device_id_type=MESH)

    pl.semaphore_wait(barrier, jnp.where(at_end, 7, 6))

    def core_copy(src, dst, n):
        return pltpu.make_async_remote_copy(
            src_ref=src, dst_ref=dst, send_sem=core_send.at[n], recv_sem=core_recv.at[n],
            device_id=dev_core, device_id_type=MESH)

    cores = [
        core_copy(q_ref.at[:, q_cols(other)], qbuf.at[c], 0),
        core_copy(stage_s, kv.at[c, z, x], 1),
    ]
    cores[0].start()

    sends = []

    def send(src, dst, dev, cond=None, inside=None):
        place = len(sends)

        def copy():
            return pltpu.make_async_remote_copy(
                src_ref=kv.at[src], dst_ref=kv.at[dst], send_sem=ss.at[place],
                recv_sem=rs.at[dst], device_id=dev, device_id_type=MESH)

        sends.append((copy, [one for one in (cond, inside) if one is not None]))
        if cond is None:
            copy().start()
        else:
            pl.when(cond)(lambda: copy().start())

    def arrived(slot):
        pltpu.make_async_remote_copy(
            src_ref=kv.at[slot], dst_ref=kv.at[slot], send_sem=ss.at[0],
            recv_sem=rs.at[slot], device_id=dev_xr, device_id_type=MESH).wait_recv()

    first_row, not_first, not_last = row == 0, row != 0, row != 7

    def up(src, kind, inside=None):
        send(src, (kind,) + src[1:], dev_up, not_last, inside)

    def own(t):
        for half in range(2):
            slot = (t, z, x, half)
            for dev in (dev_xr, dev_xl, dev_z):
                send(slot, slot, dev)
            up(slot, t + 2)

    def fill(dst, half):
        for g in range(GROUPS):
            cols = pl.ds(pl.multiple_of((half * GROUPS + g) * HEAD, HEAD), HEAD)
            dst[g // 2, 0, g % 2] = kin[:, cols].astype(jnp.float32).T.astype(jnp.bfloat16)
            dst[g // 2, 1, g % 2] = vin[:, cols]

    for copy in locals_[:2]:
        copy.wait()
    fill(stage_s, other)
    cores[1].start()
    fill(kv.at[c, z, x], c)
    own(c)
    cores[1].wait_recv()
    own(other)

    tt = lax.broadcasted_iota(jnp.int32, (TOK, TOK), 0)
    kk = lax.broadcasted_iota(jnp.int32, (TOK, TOK), 1)
    bias_s[...] = jnp.where(kk <= tt, 0.0, -FAR)

    locals_[3].wait()

    def start_of(i):
        total, first = len_ref[0] * 0, len_ref[0] * 0
        for r in range(8):
            total = total + len_ref[r]
            first = jnp.where(total <= i, total, first)
        return first

    start0, start1 = start_of(2 * row), start_of(2 * row + 1)

    def fine(start, key_inst):
        return jnp.where(start <= key_inst, 0.0, FAR).astype(jnp.float32)

    z1o, z2o = 1 - z1, 1 - z2
    places = {"x": x, "xl": xl, "xr": xr, "xx": xx}

    def slot_of(t, near, place):
        home, away = (z, zo) if t < 2 else (z1, z1o) if t < 4 else (z2, z2o)
        return (t, home if near else away, places[place])

    def event(t, near, place, half):
        slot = slot_of(t, near, place) + (half,)
        inside = None if t < 2 else not_first
        on = lambda *devs: [send(slot, slot, dev, None, inside) for dev in devs]
        arrived(slot)
        if not near:
            if place == "x":
                on(dev_xr, dev_xl)
        elif t < 2:
            if place == "xx":
                on(dev_z)
            elif (t, place) == (0, "xl"):
                on(dev_xr)
            elif (t, place) == (1, "xr"):
                on(dev_xl)
            up(slot, t + 2)
        elif t < 4:
            if place in ("x", "xx"):
                on(dev_z)
            if (t, place) == (3, "x"):
                up(slot, 4, not_first)
        elif place == "x":
            on(dev_xr, dev_xl, dev_z)
        elif place == "xl":
            on(dev_xr)
        elif place == "xx":
            on(dev_z)

    def relay(piece):
        for at, t, place, half in RELAY:
            if at != piece:
                continue
            slot = (t, z, places[place], half)
            arrived(slot)
            send(slot, slot, dev_outer, None, first_row)
            if (t, place) == (3, "x"):
                up(slot, 4, first_row)

    def events_at(piece):
        if any(one[0] == piece for one in RELAY):
            pl.when(first_row)(lambda: relay(piece))
        here = [one[1:] for one in EVENTS if one[0] == piece]
        for common, run_ in itertools.groupby(here, key=lambda one: one[0] < 2):
            several = list(run_)

            def go():
                for one in several:
                    event(*one)

            if common:
                go()
            else:
                pl.when(not_first)(go)

    own_even = fine(start1, 2 * row)
    flags = {(qp, t): fine((start0, start1)[qp], 2 * row + back)
             for qp in range(2) for t, back in ((2, -2), (3, -1), (4, -3))}
    earlier = {
        (near, place): jnp.where(places[place] * 2 + (z if near else zo) < b, 0.0, -FAR).astype(jnp.float32)
        for near in (True, False) for place in places}

    def tiles_of(job, qp):
        tiles = []
        for t, near, place in job:
            slot = slot_of(t, near, place)
            if t == 0 and qp == 1:
                tiles.append((slot, own_even, None))
            elif t == qp:
                tiles.append((slot, None, "own" if near and place == "x" else earlier[near, place]))
            elif t in (2, 3) or (t == 4 and qp == 0):
                tiles.append((slot, flags[qp, t], None))
        return tiles

    def run(number, job, everywhere=False, final=False):
        first = number == 0
        units = [(gg, hb, qp, tiles_of(job, qp)) for gg in range(2) for qp in range(2) for hb in range(8 // HB)]
        units = [unit for unit in units if unit[3]]

        def compute(pair):
            def head_cols(g, hb, h):
                return pl.ds(pl.multiple_of((g * 8 + hb * HB + h) * HEAD, HEAD), HEAD)

            def wide_cols(g, hb, h):
                return pl.ds(pl.multiple_of((g * 8 + hb * HB + h) * (2 * HEAD), 2 * HEAD), 2 * HEAD)

            def scores(unit):
                gg, hb, qp, tiles = unit
                g = pair * 2 + gg
                q = jnp.concatenate([qs[qp, :, wide_cols(g, hb, h)] for h in range(HB)], axis=0)
                k = jnp.concatenate([kv[slot + (pair, 0, gg)] for slot, _, _ in tiles], axis=1)
                got = jnp.dot(q, jnp.concatenate([k, k], axis=0), preferred_element_type=jnp.float32)
                out = []
                for n, (_, _, add) in enumerate(tiles):
                    sc = got[:, n * HEAD:(n + 1) * HEAD]
                    if isinstance(add, str):
                        sc = (sc.reshape(HB, TOK, TOK) + bias_s[...][None]).reshape(ROWS, TOK)
                    elif add is not None:
                        sc = sc + add
                    out.append(sc)
                return out

            def fold(unit, scs):
                gg, hb, qp, tiles = unit
                g = pair * 2 + gg
                span = pl.ds(hb * ROWS, ROWS)
                state = g * 2 + qp
                groups = {}
                for sc, (_, pen, _) in zip(scs, tiles):
                    groups.setdefault(id(pen), (pen, []))[1].append(sc)
                best = None
                for pen, members in groups.values():
                    top = members[0]
                    for one in members[1:]:
                        top = jnp.maximum(top, one)
                    top = jnp.max(top, axis=-1, keepdims=True)
                    top = top if pen is None else top - pen
                    best = top if best is None else jnp.maximum(best, top)
                best = jnp.broadcast_to(best, (ROWS, HEAD))
                if not first:
                    old = m_s[state, span, :]
                    best = jnp.maximum(old, best)
                    factor = jnp.exp2(old - best)
                shifts = {key: best if pen is None else best + pen for key, (pen, _) in groups.items()}
                ws = [jnp.exp2(sc - shifts[id(pen)]) for sc, (_, pen, _) in zip(scs, tiles)]
                w = jnp.concatenate([one.astype(jnp.bfloat16) for one in ws], axis=1)
                v = jnp.concatenate([kv[slot + (pair, 1, gg)] for slot, _, _ in tiles], axis=0)
                v = jnp.concatenate([v, jnp.ones_like(v)], axis=1)
                both = jnp.dot(w, v, preferred_element_type=jnp.float32)
                part, total = both[:, :HEAD], both[:, HEAD:]
                if not first:
                    total = l_s[state, span, :] * factor + total
                    part = acc_s[state, span, :] * factor + part
                if final:
                    res = (part / total).astype(jnp.bfloat16)
                    for h in range(HB):
                        obuf[qp, :, head_cols(g, hb, h)] = res[h * TOK:(h + 1) * TOK]
                else:
                    m_s[state, span, :] = best
                    l_s[state, span, :] = total
                    acc_s[state, span, :] = part

            ahead = scores(units[0])
            for n, unit in enumerate(units):
                scs = ahead
                if n + 1 < len(units):
                    ahead = scores(units[n + 1])
                fold(unit, scs)
                if final and unit[0] != (units + [(None,)])[n + 1][0]:
                    for copy in results(pair * 2 + unit[0]):
                        copy.start()

        def body(pair, carry):
            if any(e[0] == number * 2 + 1 for e in EVENTS + RELAY):
                pl.when(pair == 1)(lambda: events_at(number * 2 + 1))
            if everywhere:
                compute(pair)
            else:
                pl.when(not_first)(lambda: compute(pair))
            return carry

        events_at(number * 2)
        lax.fori_loop(0, 2, body, 0)

    def results(g):
        cols = pl.ds(pl.multiple_of(g * (8 * HEAD), HEAD), 8 * HEAD)
        ocols = pl.ds(pl.multiple_of((c * GROUPS + g) * (8 * HEAD), HEAD), 8 * HEAD)
        return (
            pltpu.make_async_copy(obuf.at[c, :, cols], o_ref.at[:, ocols], osem.at[0, g]),
            pltpu.make_async_remote_copy(
                src_ref=obuf.at[other, :, cols], dst_ref=o_ref.at[:, ocols],
                send_sem=osem.at[1, g], recv_sem=osem.at[2, g],
                device_id=dev_core, device_id_type=MESH),
        )

    locals_[2].wait()
    cores[0].wait_recv()

    def scale(h, carry):
        for qp in range(2):
            q = qbuf[qp, :, pl.ds(pl.multiple_of(h * HEAD, HEAD), HEAD)].astype(jnp.float32) * SCALE
            high = q.astype(jnp.bfloat16)
            low = (q - high.astype(jnp.float32)).astype(jnp.bfloat16)
            qs[qp, :, pl.ds(pl.multiple_of(h * (2 * HEAD), HEAD), HEAD)] = high
            qs[qp, :, pl.ds(pl.multiple_of(h * (2 * HEAD) + HEAD, HEAD), HEAD)] = low
        return carry

    lax.fori_loop(0, 8 * GROUPS, scale, 0, unroll=4)
    shared = [job[0][0] < 2 for job in JOBS]
    last_shared = max(n for n, one in enumerate(shared) if one)
    for number in range(last_shared + 1):
        run(number, JOBS[number], everywhere=shared[number])

    @pl.when(first_row)
    def _():
        def body(g, carry):
            for qp in range(2):
                for h in range(8):
                    span = pl.ds(h * TOK, TOK)
                    total = l_s[g * 2 + qp, span, :]
                    cols = pl.ds(pl.multiple_of((g * 8 + h) * HEAD, HEAD), HEAD)
                    obuf[qp, :, cols] = (acc_s[g * 2 + qp, span, :] / total).astype(jnp.bfloat16)
            for copy in results(g):
                copy.start()
            return carry

        lax.fori_loop(0, GROUPS, body, 0)

    for number in range(last_shared + 1, len(JOBS)):
        run(number, JOBS[number], final=number == len(JOBS) - 1)

    assert len(sends) <= 112
    for copy, conds in sends:
        if conds:
            cond = conds[0] if len(conds) == 1 else jnp.logical_and(*conds)
            pl.when(cond)(lambda copy=copy: copy().wait_send())
        else:
            copy().wait_send()
    for copy in cores:
        copy.wait_send()
    for g in range(GROUPS):
        mine, theirs = results(g)
        mine.wait()
        theirs.wait()


def local(queries, keys, values, lengths):
    dma = pltpu.SemaphoreType.DMA
    anywhere = pl.BlockSpec(memory_space=pl.ANY)
    queries, keys, values, lengths = (
        pltpu.with_memory_space_constraint(one, pltpu.HBM) for one in (queries, keys, values, lengths))
    return pl.pallas_call(
        kernel,
        out_shape=jax.ShapeDtypeStruct(queries.shape, jnp.bfloat16),
        in_specs=[anywhere] * 4,
        out_specs=anywhere,
        scratch_shapes=[
            pltpu.VMEM((5, 2, 4, 2, 2, 2, TOK, HEAD), jnp.bfloat16),
            pltpu.VMEM((2, 2, 2, TOK, HEAD), jnp.bfloat16),
            pltpu.VMEM((TOK, 2 * HALF), jnp.bfloat16),
            pltpu.VMEM((TOK, 2 * HALF), jnp.bfloat16),
            pltpu.VMEM((2, TOK, 8 * HALF), jnp.bfloat16),
            pltpu.VMEM((2, TOK, 16 * HALF), jnp.bfloat16),
            pltpu.VMEM((2, TOK, 8 * HALF), jnp.bfloat16),
            pltpu.VMEM((2 * GROUPS, 8 * TOK, HEAD), jnp.float32),
            pltpu.VMEM((2 * GROUPS, 8 * TOK, HEAD), jnp.float32),
            pltpu.VMEM((2 * GROUPS, 8 * TOK, HEAD), jnp.float32),
            pltpu.VMEM((TOK, TOK), jnp.float32),
            pltpu.SMEM((8,), jnp.int32),
            dma((5, 2, 4, 2)),
            dma((112,)),
            dma((4,)),
            dma((2,)),
            dma((2,)),
            dma((3, GROUPS)),
        ],
        compiler_params=pltpu.CompilerParams(
            collective_id=0, has_side_effects=True, vmem_limit_bytes=44 * 1024 * 1024),
        cost_estimate=pl.CostEstimate(flops=30_000_000_000, bytes_accessed=8_000_000, transcendentals=40_000_000),
    )(lengths, queries, keys, values)


def solution(mesh):
    split = P(("inst", "blk"), None)
    return jax.shard_map(local, mesh=mesh, in_specs=(split, split, split, P()), out_specs=split, check_vma=False)
```

```python
import itertools
import math

import jax
import jax.numpy as jnp
from jax import lax
from jax.experimental import pallas as pl
from jax.experimental.pallas import tpu as pltpu
from jax.sharding import PartitionSpec as P

MESH = pl.DeviceIdType.MESH
HEAD = 128
TOK = 128
GROUPS = 4
HB = 4
ROWS = HB * TOK
HALF = GROUPS * HEAD
SCALE = HEAD**-0.5 * math.log2(math.e)
FAR = 1e30

JOBS = (
    ((0, True, "x"), (1, True, "x"),),
    ((0, True, "xl"), (0, True, "xr"), (0, False, "x"),),
    ((1, True, "xl"), (1, True, "xr"), (1, False, "x"),),
    ((2, True, "x"), (3, True, "x"), (2, False, "x"), (3, False, "x"),),
    ((0, False, "xl"), (0, False, "xr"), (0, True, "xx"), (1, False, "xl"), (1, False, "xr"), (1, True, "xx"),),
    ((0, False, "xx"), (1, False, "xx"),),
    ((2, True, "xl"), (2, True, "xr"), (3, True, "xl"), (3, True, "xr"), (4, True, "x"), (4, False, "x"),),
    ((2, False, "xl"), (2, False, "xr"), (3, False, "xl"), (3, False, "xr"), (4, True, "xl"), (4, True, "xr"),),
    ((2, True, "xx"), (3, True, "xx"), (4, True, "xx"), (4, False, "xl"), (4, False, "xr"),),
    ((2, False, "xx"), (3, False, "xx"), (4, False, "xx"),),
)
EVENTS = (
    (0, 2, True, "x", 0),
    (0, 0, False, "x", 1),
    (0, 2, True, "x", 1),
    (0, 0, False, "x", 0),
    (1, 3, True, "x", 0),
    (1, 0, True, "xl", 1),
    (1, 1, True, "xr", 0),
    (1, 0, True, "xl", 0),
    (1, 1, False, "x", 1),
    (1, 1, True, "xr", 1),
    (2, 3, True, "x", 1),
    (2, 0, True, "xr", 0),
    (2, 0, True, "xr", 1),
    (3, 1, True, "xl", 0),
    (3, 1, True, "xl", 1),
    (3, 0, False, "xl", 1),
    (4, 4, True, "x", 0),
    (4, 0, True, "xx", 1),
    (4, 0, False, "xr", 0),
    (4, 1, False, "x", 0),
    (4, 3, False, "x", 0),
    (5, 0, True, "xx", 0),
    (6, 3, True, "xr", 0),
    (6, 2, False, "x", 0),
    (7, 2, False, "x", 1),
    (7, 1, True, "xx", 0),
    (7, 1, False, "xl", 1),
    (7, 0, False, "xr", 1),
    (7, 2, True, "xl", 0),
    (7, 1, True, "xx", 1),
    (7, 2, True, "xl", 1),
    (7, 0, False, "xl", 0),
    (7, 1, False, "xr", 1),
    (7, 4, True, "xl", 0),
    (7, 3, False, "x", 1),
    (8, 0, False, "xx", 0),
    (8, 1, False, "xr", 0),
    (8, 1, False, "xl", 0),
    (10, 0, False, "xx", 1),
    (10, 4, True, "x", 1),
    (10, 1, False, "xx", 0),
    (10, 4, False, "x", 0),
    (10, 2, True, "xr", 0),
    (11, 3, True, "xr", 1),
    (11, 1, False, "xx", 1),
    (12, 3, True, "xl", 0),
    (12, 2, False, "xl", 1),
    (12, 3, False, "xr", 0),
    (13, 4, True, "xx", 0),
    (13, 3, True, "xl", 1),
    (13, 2, True, "xr", 1),
    (13, 4, False, "x", 1),
    (14, 2, True, "xx", 1),
    (14, 2, False, "xr", 0),
    (14, 4, True, "xr", 1),
    (14, 4, True, "xr", 0),
    (14, 4, False, "xx", 0),
    (14, 3, False, "xr", 1),
    (14, 2, False, "xl", 0),
    (14, 3, False, "xl", 1),
    (14, 4, False, "xr", 0),
    (14, 2, False, "xr", 1),
    (14, 4, True, "xl", 1),
    (14, 3, False, "xl", 0),
    (14, 2, True, "xx", 0),
    (15, 3, True, "xx", 0),
    (15, 2, False, "xx", 1),
    (15, 4, False, "xr", 1),
    (16, 4, False, "xl", 1),
    (16, 3, True, "xx", 1),
    (16, 2, False, "xx", 0),
    (16, 4, False, "xl", 0),
    (17, 3, False, "xx", 0),
    (17, 4, True, "xx", 1),
    (19, 3, False, "xx", 1),
    (19, 4, False, "xx", 1),
)
RELAY = (
    (0, 2, "x", 0),
    (0, 2, "x", 1),
    (0, 3, "x", 0),
    (1, 3, "x", 1),
    (1, 4, "x", 0),
    (2, 2, "xl", 1),
    (2, 3, "xr", 0),
    (2, 2, "xl", 0),
    (3, 3, "xr", 1),
    (3, 4, "x", 1),
    (4, 2, "xr", 0),
    (4, 2, "xr", 1),
    (5, 3, "xl", 0),
    (7, 3, "xl", 1),
    (7, 2, "xx", 1),
    (8, 2, "xx", 0),
    (9, 3, "xx", 0),
    (10, 3, "xx", 1),
)


def kernel(len_hbm, q_ref, k_ref, v_ref, o_ref, kv, stage_s, kin, vin, qbuf, qs, obuf, acc_s, m_s, l_s, bias_s,
           len_ref, rs, ss, loc, core_send, core_recv, osem):
    inst, b = lax.axis_index("inst"), lax.axis_index("blk")
    c, row = lax.rem(inst, 2), inst // 2
    other = 1 - c
    z, x = lax.rem(b, 2), b // 2
    zo = 1 - z
    xr, xl, xx = lax.rem(x + 1, 4), lax.rem(x + 3, 4), lax.rem(x + 2, 4)
    dev_xr, dev_xl = (inst, xr * 2 + z), (inst, xl * 2 + z)
    dev_z = (inst, x * 2 + zo)
    dev_core = (inst + 1 - 2 * c, b)
    y, zh = lax.rem(row, 4), row // 4
    dev_up = ((zh * 4 + lax.rem(y + 1, 4)) * 2 + c, b)
    dev_down = ((zh * 4 + lax.rem(y + 3, 4)) * 2 + c, b)
    dev_outer = ((4 - row) * 2 + c, x * 2 + zo)
    at_end = jnp.logical_or(row == 0, row == 4)
    z1 = jnp.where(row == 4, zo, z)
    z2 = jnp.where(jnp.logical_or(row == 4, row == 5), zo, z)

    q_cols = lambda half: pl.ds(pl.multiple_of(half * (8 * HALF), HEAD), 8 * HALF)
    locals_ = [
        pltpu.make_async_copy(k_ref, kin, loc.at[0]),
        pltpu.make_async_copy(v_ref, vin, loc.at[1]),
        pltpu.make_async_copy(q_ref.at[:, q_cols(c)], qbuf.at[c], loc.at[2]),
        pltpu.make_async_copy(len_hbm, len_ref, loc.at[3]),
    ]
    for copy in locals_:
        copy.start()

    barrier = pltpu.get_barrier_semaphore()
    for dev in (dev_xr, dev_xl, dev_z, dev_core, dev_up, dev_down):
        pl.semaphore_signal(barrier, inc=1, device_id=dev, device_id_type=MESH)

    @pl.when(at_end)
    def _():
        pl.semaphore_signal(barrier, inc=1, device_id=dev_outer, device_id_type=MESH)

    pl.semaphore_wait(barrier, jnp.where(at_end, 7, 6))

    def core_copy(src, dst, n):
        return pltpu.make_async_remote_copy(
            src_ref=src, dst_ref=dst, send_sem=core_send.at[n], recv_sem=core_recv.at[n],
            device_id=dev_core, device_id_type=MESH)

    cores = [
        core_copy(q_ref.at[:, q_cols(other)], qbuf.at[c], 0),
        core_copy(stage_s, kv.at[c, z, x], 1),
    ]
    cores[0].start()

    sends, drained, job_now = [], [0], [0]

    def drain(before):
        while drained[0] < len(sends) and sends[drained[0]][2] < before:
            copy, conds, _ = sends[drained[0]]
            drained[0] += 1
            if conds:
                cond = conds[0] if len(conds) == 1 else jnp.logical_and(*conds)
                pl.when(cond)(lambda: copy().wait_send())
            else:
                copy().wait_send()

    def send(src, dst, dev, cond=None, inside=None):
        place = len(sends)

        def copy():
            return pltpu.make_async_remote_copy(
                src_ref=kv.at[src], dst_ref=kv.at[dst], send_sem=ss.at[place],
                recv_sem=rs.at[dst], device_id=dev, device_id_type=MESH)

        sends.append((copy, [one for one in (cond, inside) if one is not None], job_now[0]))
        if cond is None:
            copy().start()
        else:
            pl.when(cond)(lambda: copy().start())

    def arrived(slot):
        pltpu.make_async_remote_copy(
            src_ref=kv.at[slot], dst_ref=kv.at[slot], send_sem=ss.at[0],
            recv_sem=rs.at[slot], device_id=dev_xr, device_id_type=MESH).wait_recv()

    first_row, not_first, not_last = row == 0, row != 0, row != 7

    def up(src, kind, inside=None):
        send(src, (kind,) + src[1:], dev_up, not_last, inside)

    def own(t):
        for half in range(2):
            slot = (t, z, x, half)
            for dev in (dev_xr, dev_xl, dev_z):
                send(slot, slot, dev)
            up(slot, t + 2)

    def fill(dst, half):
        for g in range(GROUPS):
            cols = pl.ds(pl.multiple_of((half * GROUPS + g) * HEAD, HEAD), HEAD)
            dst[g // 2, 0, g % 2] = kin[:, cols].astype(jnp.float32).T.astype(jnp.bfloat16)
            dst[g // 2, 1, g % 2] = vin[:, cols]

    for copy in locals_[:2]:
        copy.wait()
    fill(kv.at[c, z, x], c)
    own(c)
    fill(stage_s, other)
    cores[1].start()
    cores[1].wait_recv()
    own(other)

    tt = lax.broadcasted_iota(jnp.int32, (TOK, TOK), 0)
    kk = lax.broadcasted_iota(jnp.int32, (TOK, TOK), 1)
    bias_s[...] = jnp.where(kk <= tt, 0.0, -FAR)

    locals_[3].wait()

    def start_of(i):
        total, first = len_ref[0] * 0, len_ref[0] * 0
        for r in range(8):
            total = total + len_ref[r]
            first = jnp.where(total <= i, total, first)
        return first

    start0, start1 = start_of(2 * row), start_of(2 * row + 1)

    def fine(start, key_inst):
        return jnp.where(start <= key_inst, 0.0, FAR).astype(jnp.float32)

    z1o, z2o = 1 - z1, 1 - z2
    places = {"x": x, "xl": xl, "xr": xr, "xx": xx}

    def slot_of(t, near, place):
        home, away = (z, zo) if t < 2 else (z1, z1o) if t < 4 else (z2, z2o)
        return (t, home if near else away, places[place])

    def event(t, near, place, half):
        slot = slot_of(t, near, place) + (half,)
        inside = None if t < 2 else not_first
        on = lambda *devs: [send(slot, slot, dev, None, inside) for dev in devs]
        arrived(slot)
        if not near:
            if place == "x":
                on(dev_xr, dev_xl)
        elif t < 2:
            if place == "xx":
                on(dev_z)
            elif (t, place) == (0, "xl"):
                on(dev_xr)
            elif (t, place) == (1, "xr"):
                on(dev_xl)
            up(slot, t + 2)
        elif t < 4:
            if place in ("x", "xx"):
                on(dev_z)
            if (t, place) == (3, "x"):
                up(slot, 4, not_first)
        elif place == "x":
            on(dev_xr, dev_xl, dev_z)
        elif place == "xl":
            on(dev_xr)
        elif place == "xx":
            on(dev_z)

    def relay(piece):
        for at, t, place, half in RELAY:
            if at != piece:
                continue
            slot = (t, z, places[place], half)
            arrived(slot)
            send(slot, slot, dev_outer, None, first_row)
            if (t, place) == (3, "x"):
                up(slot, 4, first_row)

    def events_at(piece):
        if any(one[0] == piece for one in RELAY):
            pl.when(first_row)(lambda: relay(piece))
        here = [one[1:] for one in EVENTS if one[0] == piece]
        for common, run_ in itertools.groupby(here, key=lambda one: one[0] < 2):
            several = list(run_)

            def go():
                for one in several:
                    event(*one)

            if common:
                go()
            else:
                pl.when(not_first)(go)

    own_even = fine(start1, 2 * row)
    flags = {(qp, t): fine((start0, start1)[qp], 2 * row + back)
             for qp in range(2) for t, back in ((2, -2), (3, -1), (4, -3))}
    earlier = {
        (near, place): jnp.where(places[place] * 2 + (z if near else zo) < b, 0.0, -FAR).astype(jnp.float32)
        for near in (True, False) for place in places}

    def tiles_of(job, qp):
        tiles = []
        for t, near, place in job:
            slot = slot_of(t, near, place)
            if t == 0 and qp == 1:
                tiles.append((slot, own_even, None))
            elif t == qp:
                tiles.append((slot, None, "own" if near and place == "x" else earlier[near, place]))
            elif t in (2, 3) or (t == 4 and qp == 0):
                tiles.append((slot, flags[qp, t], None))
        return tiles

    def run(number, job, everywhere=False, final=False):
        first = number == 0
        units = [(gg, hb, qp, tiles_of(job, qp)) for gg in range(2) for qp in range(2) for hb in range(8 // HB)]
        units = [unit for unit in units if unit[3]]

        def compute(pair):
            def head_cols(g, hb, h):
                return pl.ds(pl.multiple_of((g * 8 + hb * HB + h) * HEAD, HEAD), HEAD)

            def wide_cols(g, hb, h):
                return pl.ds(pl.multiple_of((g * 8 + hb * HB + h) * (2 * HEAD), 2 * HEAD), 2 * HEAD)

            def scores(unit):
                gg, hb, qp, tiles = unit
                g = pair * 2 + gg
                q = jnp.concatenate([qs[qp, :, wide_cols(g, hb, h)] for h in range(HB)], axis=0)
                k = jnp.concatenate([kv[slot + (pair, 0, gg)] for slot, _, _ in tiles], axis=1)
                got = jnp.dot(q, jnp.concatenate([k, k], axis=0), preferred_element_type=jnp.float32)
                out = []
                for n, (_, _, add) in enumerate(tiles):
                    sc = got[:, n * HEAD:(n + 1) * HEAD]
                    if isinstance(add, str):
                        sc = (sc.reshape(HB, TOK, TOK) + bias_s[...][None]).reshape(ROWS, TOK)
                    elif add is not None:
                        sc = sc + add
                    out.append(sc)
                return out

            def fold(unit, scs):
                gg, hb, qp, tiles = unit
                g = pair * 2 + gg
                span = pl.ds(hb * ROWS, ROWS)
                state = g * 2 + qp
                groups = {}
                for sc, (_, pen, _) in zip(scs, tiles):
                    groups.setdefault(id(pen), (pen, []))[1].append(sc)
                best = None
                for pen, members in groups.values():
                    top = members[0]
                    for one in members[1:]:
                        top = jnp.maximum(top, one)
                    top = jnp.max(top, axis=-1, keepdims=True)
                    top = top if pen is None else top - pen
                    best = top if best is None else jnp.maximum(best, top)
                best = jnp.broadcast_to(best, (ROWS, HEAD))
                if not first:
                    old = m_s[state, span, :]
                    best = jnp.maximum(old, best)
                    factor = jnp.exp2(old - best)
                shifts = {key: best if pen is None else best + pen for key, (pen, _) in groups.items()}
                ws = [jnp.exp2(sc - shifts[id(pen)]) for sc, (_, pen, _) in zip(scs, tiles)]
                w = jnp.concatenate([one.astype(jnp.bfloat16) for one in ws], axis=1)
                v = jnp.concatenate([kv[slot + (pair, 1, gg)] for slot, _, _ in tiles], axis=0)
                v = jnp.concatenate([v, jnp.ones_like(v)], axis=1)
                both = jnp.dot(w, v, preferred_element_type=jnp.float32)
                part, total = both[:, :HEAD], both[:, HEAD:]
                if not first:
                    total = l_s[state, span, :] * factor + total
                    part = acc_s[state, span, :] * factor + part
                if final:
                    res = (part / total).astype(jnp.bfloat16)
                    for h in range(HB):
                        obuf[qp, :, head_cols(g, hb, h)] = res[h * TOK:(h + 1) * TOK]
                else:
                    m_s[state, span, :] = best
                    l_s[state, span, :] = total
                    acc_s[state, span, :] = part

            ahead = scores(units[0])
            for n, unit in enumerate(units):
                scs = ahead
                if n + 1 < len(units):
                    ahead = scores(units[n + 1])
                fold(unit, scs)
                if final and unit[0] != (units + [(None,)])[n + 1][0]:
                    for copy in results(pair * 2 + unit[0]):
                        copy.start()

        def body(pair, carry):
            if any(e[0] == number * 2 + 1 for e in EVENTS + RELAY):
                pl.when(pair == 1)(lambda: events_at(number * 2 + 1))
            if everywhere:
                compute(pair)
            else:
                pl.when(not_first)(lambda: compute(pair))
            return carry

        job_now[0] = number
        drain(number - 2)
        events_at(number * 2)
        lax.fori_loop(0, 2, body, 0)

    def results(g):
        cols = pl.ds(pl.multiple_of(g * (8 * HEAD), HEAD), 8 * HEAD)
        ocols = pl.ds(pl.multiple_of((c * GROUPS + g) * (8 * HEAD), HEAD), 8 * HEAD)
        return (
            pltpu.make_async_copy(obuf.at[c, :, cols], o_ref.at[:, ocols], osem.at[0, g]),
            pltpu.make_async_remote_copy(
                src_ref=obuf.at[other, :, cols], dst_ref=o_ref.at[:, ocols],
                send_sem=osem.at[1, g], recv_sem=osem.at[2, g],
                device_id=dev_core, device_id_type=MESH),
        )

    locals_[2].wait()
    cores[0].wait_recv()

    def scale(h, carry):
        for qp in range(2):
            q = qbuf[qp, :, pl.ds(pl.multiple_of(h * HEAD, HEAD), HEAD)].astype(jnp.float32) * SCALE
            high = q.astype(jnp.bfloat16)
            low = (q - high.astype(jnp.float32)).astype(jnp.bfloat16)
            qs[qp, :, pl.ds(pl.multiple_of(h * (2 * HEAD), HEAD), HEAD)] = high
            qs[qp, :, pl.ds(pl.multiple_of(h * (2 * HEAD) + HEAD, HEAD), HEAD)] = low
        return carry

    lax.fori_loop(0, 8 * GROUPS, scale, 0, unroll=4)
    shared = [job[0][0] < 2 for job in JOBS]
    last_shared = max(n for n, one in enumerate(shared) if one)
    for number in range(last_shared + 1):
        run(number, JOBS[number], everywhere=shared[number])

    @pl.when(first_row)
    def _():
        def body(g, carry):
            for qp in range(2):
                for h in range(8):
                    span = pl.ds(h * TOK, TOK)
                    total = l_s[g * 2 + qp, span, :]
                    cols = pl.ds(pl.multiple_of((g * 8 + h) * HEAD, HEAD), HEAD)
                    obuf[qp, :, cols] = (acc_s[g * 2 + qp, span, :] / total).astype(jnp.bfloat16)
            for copy in results(g):
                copy.start()
            return carry

        lax.fori_loop(0, GROUPS, body, 0)

    for number in range(last_shared + 1, len(JOBS)):
        run(number, JOBS[number], final=number == len(JOBS) - 1)

    assert len(sends) <= 112
    drain(len(JOBS))
    for copy in cores:
        copy.wait_send()
    for g in range(GROUPS):
        mine, theirs = results(g)
        mine.wait()
        theirs.wait()


def local(queries, keys, values, lengths):
    dma = pltpu.SemaphoreType.DMA
    anywhere = pl.BlockSpec(memory_space=pl.ANY)
    queries, keys, values, lengths = (
        pltpu.with_memory_space_constraint(one, pltpu.HBM) for one in (queries, keys, values, lengths))
    return pl.pallas_call(
        kernel,
        out_shape=jax.ShapeDtypeStruct(queries.shape, jnp.bfloat16),
        in_specs=[anywhere] * 4,
        out_specs=anywhere,
        scratch_shapes=[
            pltpu.VMEM((5, 2, 4, 2, 2, 2, TOK, HEAD), jnp.bfloat16),
            pltpu.VMEM((2, 2, 2, TOK, HEAD), jnp.bfloat16),
            pltpu.VMEM((TOK, 2 * HALF), jnp.bfloat16),
            pltpu.VMEM((TOK, 2 * HALF), jnp.bfloat16),
            pltpu.VMEM((2, TOK, 8 * HALF), jnp.bfloat16),
            pltpu.VMEM((2, TOK, 16 * HALF), jnp.bfloat16),
            pltpu.VMEM((2, TOK, 8 * HALF), jnp.bfloat16),
            pltpu.VMEM((2 * GROUPS, 8 * TOK, HEAD), jnp.float32),
            pltpu.VMEM((2 * GROUPS, 8 * TOK, HEAD), jnp.float32),
            pltpu.VMEM((2 * GROUPS, 8 * TOK, HEAD), jnp.float32),
            pltpu.VMEM((TOK, TOK), jnp.float32),
            pltpu.SMEM((8,), jnp.int32),
            dma((5, 2, 4, 2)),
            dma((112,)),
            dma((4,)),
            dma((2,)),
            dma((2,)),
            dma((3, GROUPS)),
        ],
        compiler_params=pltpu.CompilerParams(
            collective_id=0, has_side_effects=True, vmem_limit_bytes=44 * 1024 * 1024),
        cost_estimate=pl.CostEstimate(flops=30_000_000_000, bytes_accessed=8_000_000, transcendentals=40_000_000),
    )(lengths, queries, keys, values)


def solution(mesh):
    split = P(("inst", "blk"), None)
    return jax.shard_map(local, mesh=mesh, in_specs=(split, split, split, P()), out_specs=split, check_vma=False)
```

```python
import itertools
import math

import jax
import jax.numpy as jnp
from jax import lax
from jax.experimental import pallas as pl
from jax.experimental.pallas import tpu as pltpu
from jax.sharding import PartitionSpec as P

MESH = pl.DeviceIdType.MESH
HEAD = 128
TOK = 128
GROUPS = 4
HB = 4
ROWS = HB * TOK
HALF = GROUPS * HEAD
SCALE = HEAD**-0.5 * math.log2(math.e)
FAR = 1e30

JOBS = (
    ((0, True, "x"), (1, True, "x"),),
    ((0, True, "xl"), (1, True, "xl"), (0, True, "xr"), (1, True, "xr"), (0, False, "x"), (1, False, "x"),),
    ((2, True, "x"), (3, True, "x"), (2, False, "x"), (3, False, "x"),),
    ((0, False, "xl"), (0, False, "xr"), (0, True, "xx"), (0, False, "xx"), (1, False, "xl"), (1, False, "xr"), (1, True, "xx"), (1, False, "xx"),),
    ((2, True, "xl"), (2, True, "xr"), (3, True, "xl"), (3, True, "xr"),),
    ((4, True, "x"), (4, False, "x"), (4, True, "xl"), (4, True, "xr"),),
    ((2, False, "xl"), (2, False, "xr"), (3, False, "xl"), (3, False, "xr"),),
    ((4, True, "xx"), (4, False, "xx"), (4, False, "xl"), (4, False, "xr"),),
    ((2, True, "xx"), (2, False, "xx"), (3, True, "xx"), (3, False, "xx"),),
)
EVENTS = (
    (0, 0, False, "x", 1),
    (0, 0, False, "x", 0),
    (1, 2, True, "x", 1),
    (1, 2, True, "x", 0),
    (1, 0, True, "xl", 0),
    (1, 1, False, "x", 0),
    (2, 3, True, "x", 0),
    (2, 0, True, "xr", 0),
    (2, 1, True, "xr", 0),
    (2, 1, False, "x", 1),
    (2, 1, True, "xl", 0),
    (3, 3, True, "x", 1),
    (3, 0, True, "xl", 1),
    (3, 1, True, "xr", 1),
    (3, 0, True, "xr", 1),
    (3, 1, True, "xl", 1),
    (4, 0, False, "xl", 0),
    (4, 4, True, "x", 0),
    (4, 1, True, "xx", 0),
    (4, 0, False, "xl", 1),
    (4, 0, True, "xx", 0),
    (4, 2, False, "x", 0),
    (4, 3, False, "x", 0),
    (5, 2, False, "x", 1),
    (5, 1, False, "xl", 1),
    (5, 3, False, "x", 1),
    (5, 1, False, "xr", 0),
    (6, 0, False, "xr", 1),
    (6, 1, True, "xx", 1),
    (6, 1, False, "xl", 0),
    (6, 1, False, "xr", 1),
    (6, 2, True, "xr", 0),
    (6, 0, True, "xx", 1),
    (6, 0, False, "xx", 0),
    (6, 4, True, "xl", 0),
    (6, 3, True, "xr", 0),
    (6, 1, False, "xx", 0),
    (6, 0, False, "xr", 0),
    (7, 2, False, "xr", 0),
    (7, 4, True, "x", 1),
    (7, 4, False, "x", 0),
    (7, 4, True, "xr", 0),
    (7, 2, False, "xl", 0),
    (7, 0, False, "xx", 1),
    (7, 1, False, "xx", 1),
    (8, 3, True, "xr", 1),
    (8, 3, False, "xl", 0),
    (8, 3, False, "xr", 0),
    (8, 2, False, "xr", 1),
    (8, 2, True, "xl", 0),
    (8, 3, True, "xl", 0),
    (9, 2, True, "xl", 1),
    (9, 3, False, "xl", 1),
    (9, 2, False, "xl", 1),
    (9, 3, False, "xr", 1),
    (9, 2, True, "xr", 1),
    (9, 3, True, "xl", 1),
    (9, 4, True, "xx", 0),
    (10, 3, True, "xx", 0),
    (10, 4, True, "xl", 1),
    (11, 4, True, "xr", 1),
    (11, 4, False, "x", 1),
    (12, 2, True, "xx", 0),
    (13, 4, True, "xx", 1),
    (13, 4, False, "xx", 0),
    (14, 2, True, "xx", 1),
    (14, 4, False, "xl", 0),
    (14, 4, False, "xr", 0),
    (15, 4, False, "xl", 1),
    (15, 3, True, "xx", 1),
    (15, 4, False, "xx", 1),
    (15, 4, False, "xr", 1),
    (16, 3, False, "xx", 0),
    (16, 2, False, "xx", 0),
    (17, 2, False, "xx", 1),
    (17, 3, False, "xx", 1),
)
RELAY = (
    (0, 2, "x", 0),
    (0, 2, "x", 1),
    (0, 3, "x", 0),
    (1, 3, "x", 1),
    (1, 2, "xl", 0),
    (1, 4, "x", 0),
    (1, 2, "xr", 0),
    (2, 3, "xr", 0),
    (3, 3, "xl", 0),
    (3, 4, "x", 1),
    (4, 2, "xl", 1),
    (5, 3, "xr", 1),
    (5, 2, "xr", 1),
    (6, 3, "xl", 1),
    (6, 3, "xx", 0),
    (7, 2, "xx", 0),
    (7, 3, "xx", 1),
    (7, 2, "xx", 1),
)


def kernel(len_hbm, q_ref, k_ref, v_ref, o_ref, kv, stage_s, kin, vin, qbuf, qs, obuf, acc_s, m_s, l_s, bias_s,
           len_ref, rs, ss, loc, core_send, core_recv, osem):
    inst, b = lax.axis_index("inst"), lax.axis_index("blk")
    c, row = lax.rem(inst, 2), inst // 2
    other = 1 - c
    z, x = lax.rem(b, 2), b // 2
    zo = 1 - z
    xr, xl, xx = lax.rem(x + 1, 4), lax.rem(x + 3, 4), lax.rem(x + 2, 4)
    dev_xr, dev_xl = (inst, xr * 2 + z), (inst, xl * 2 + z)
    dev_z = (inst, x * 2 + zo)
    dev_core = (inst + 1 - 2 * c, b)
    y, zh = lax.rem(row, 4), row // 4
    dev_up = ((zh * 4 + lax.rem(y + 1, 4)) * 2 + c, b)
    dev_down = ((zh * 4 + lax.rem(y + 3, 4)) * 2 + c, b)
    dev_outer = ((4 - row) * 2 + c, x * 2 + zo)
    at_end = jnp.logical_or(row == 0, row == 4)
    z1 = jnp.where(row == 4, zo, z)
    z2 = jnp.where(jnp.logical_or(row == 4, row == 5), zo, z)

    q_cols = lambda half: pl.ds(pl.multiple_of(half * (8 * HALF), HEAD), 8 * HALF)
    locals_ = [
        pltpu.make_async_copy(k_ref, kin, loc.at[0]),
        pltpu.make_async_copy(v_ref, vin, loc.at[1]),
        pltpu.make_async_copy(q_ref.at[:, q_cols(c)], qbuf.at[c], loc.at[2]),
        pltpu.make_async_copy(len_hbm, len_ref, loc.at[3]),
    ]
    for copy in locals_:
        copy.start()

    barrier = pltpu.get_barrier_semaphore()
    for dev in (dev_xr, dev_xl, dev_z, dev_core, dev_up, dev_down):
        pl.semaphore_signal(barrier, inc=1, device_id=dev, device_id_type=MESH)

    @pl.when(at_end)
    def _():
        pl.semaphore_signal(barrier, inc=1, device_id=dev_outer, device_id_type=MESH)

    pl.semaphore_wait(barrier, jnp.where(at_end, 7, 6))

    def core_copy(src, dst, n):
        return pltpu.make_async_remote_copy(
            src_ref=src, dst_ref=dst, send_sem=core_send.at[n], recv_sem=core_recv.at[n],
            device_id=dev_core, device_id_type=MESH)

    cores = [
        core_copy(q_ref.at[:, q_cols(other)], qbuf.at[c], 0),
        core_copy(stage_s, kv.at[c, z, x], 1),
    ]
    cores[0].start()

    sends, drained, job_now = [], [0], [0]

    def drain(before):
        while drained[0] < len(sends) and sends[drained[0]][2] < before:
            copy, conds, _ = sends[drained[0]]
            drained[0] += 1
            if conds:
                cond = conds[0] if len(conds) == 1 else jnp.logical_and(*conds)
                pl.when(cond)(lambda: copy().wait_send())
            else:
                copy().wait_send()

    def send(src, dst, dev, cond=None, inside=None):
        place = len(sends)

        def copy():
            return pltpu.make_async_remote_copy(
                src_ref=kv.at[src], dst_ref=kv.at[dst], send_sem=ss.at[place],
                recv_sem=rs.at[dst], device_id=dev, device_id_type=MESH)

        sends.append((copy, [one for one in (cond, inside) if one is not None], job_now[0]))
        if cond is None:
            copy().start()
        else:
            pl.when(cond)(lambda: copy().start())

    def arrived(slot):
        pltpu.make_async_remote_copy(
            src_ref=kv.at[slot], dst_ref=kv.at[slot], send_sem=ss.at[0],
            recv_sem=rs.at[slot], device_id=dev_xr, device_id_type=MESH).wait_recv()

    first_row, not_first, not_last = row == 0, row != 0, row != 7

    def up(src, kind, inside=None):
        send(src, (kind,) + src[1:], dev_up, not_last, inside)

    def own(t):
        for half in range(2):
            slot = (t, z, x, half)
            for dev in (dev_xr, dev_xl, dev_z):
                send(slot, slot, dev)
            up(slot, t + 2)

    def fill(dst, half):
        for g in range(GROUPS):
            cols = pl.ds(pl.multiple_of((half * GROUPS + g) * HEAD, HEAD), HEAD)
            dst[g // 2, 0, g % 2] = kin[:, cols].astype(jnp.float32).T.astype(jnp.bfloat16)
            dst[g // 2, 1, g % 2] = vin[:, cols]

    for copy in locals_[:2]:
        copy.wait()
    fill(kv.at[c, z, x], c)
    own(c)
    fill(stage_s, other)
    cores[1].start()
    cores[1].wait_recv()
    own(other)

    tt = lax.broadcasted_iota(jnp.int32, (TOK, TOK), 0)
    kk = lax.broadcasted_iota(jnp.int32, (TOK, TOK), 1)
    bias_s[...] = jnp.where(kk <= tt, 0.0, -FAR)

    locals_[3].wait()

    def start_of(i):
        total, first = len_ref[0] * 0, len_ref[0] * 0
        for r in range(8):
            total = total + len_ref[r]
            first = jnp.where(total <= i, total, first)
        return first

    start0, start1 = start_of(2 * row), start_of(2 * row + 1)

    def fine(start, key_inst):
        return jnp.where(start <= key_inst, 0.0, FAR).astype(jnp.float32)

    z1o, z2o = 1 - z1, 1 - z2
    places = {"x": x, "xl": xl, "xr": xr, "xx": xx}

    def slot_of(t, near, place):
        home, away = (z, zo) if t < 2 else (z1, z1o) if t < 4 else (z2, z2o)
        return (t, home if near else away, places[place])

    def event(t, near, place, half):
        slot = slot_of(t, near, place) + (half,)
        inside = None if t < 2 else not_first
        on = lambda *devs: [send(slot, slot, dev, None, inside) for dev in devs]
        arrived(slot)
        if not near:
            if place == "x":
                on(dev_xr, dev_xl)
        elif t < 2:
            if place == "xx":
                on(dev_z)
            elif (t, place) == (0, "xl"):
                on(dev_xr)
            elif (t, place) == (1, "xr"):
                on(dev_xl)
            up(slot, t + 2)
        elif t < 4:
            if place in ("x", "xx"):
                on(dev_z)
            if (t, place) == (3, "x"):
                up(slot, 4, not_first)
        elif place == "x":
            on(dev_xr, dev_xl, dev_z)
        elif place == "xl":
            on(dev_xr)
        elif place == "xx":
            on(dev_z)

    def relay(piece):
        for at, t, place, half in RELAY:
            if at != piece:
                continue
            slot = (t, z, places[place], half)
            arrived(slot)
            send(slot, slot, dev_outer, None, first_row)
            if (t, place) == (3, "x"):
                up(slot, 4, first_row)

    def events_at(piece):
        if any(one[0] == piece for one in RELAY):
            pl.when(first_row)(lambda: relay(piece))
        here = [one[1:] for one in EVENTS if one[0] == piece]
        for common, run_ in itertools.groupby(here, key=lambda one: one[0] < 2):
            several = list(run_)

            def go():
                for one in several:
                    event(*one)

            if common:
                go()
            else:
                pl.when(not_first)(go)

    own_even = fine(start1, 2 * row)
    flags = {(qp, t): fine((start0, start1)[qp], 2 * row + back)
             for qp in range(2) for t, back in ((2, -2), (3, -1), (4, -3))}
    earlier = {
        (near, place): jnp.where(places[place] * 2 + (z if near else zo) < b, 0.0, -FAR).astype(jnp.float32)
        for near in (True, False) for place in places}

    def tiles_of(job, qp):
        tiles = []
        for t, near, place in job:
            slot = slot_of(t, near, place)
            if t == 0 and qp == 1:
                tiles.append((slot, own_even, None))
            elif t == qp:
                tiles.append((slot, None, "own" if near and place == "x" else earlier[near, place]))
            elif t in (2, 3) or (t == 4 and qp == 0):
                tiles.append((slot, flags[qp, t], None))
        return tiles

    def run(number, job, everywhere=False, final=False):
        first = number == 0
        units = [(gg, hb, qp, tiles_of(job, qp)) for gg in range(2) for qp in range(2) for hb in range(8 // HB)]
        units = [unit for unit in units if unit[3]]

        def compute(pair):
            def head_cols(g, hb, h):
                return pl.ds(pl.multiple_of((g * 8 + hb * HB + h) * HEAD, HEAD), HEAD)

            def wide_cols(g, hb, h):
                return pl.ds(pl.multiple_of((g * 8 + hb * HB + h) * (2 * HEAD), 2 * HEAD), 2 * HEAD)

            def scores(unit):
                gg, hb, qp, tiles = unit
                g = pair * 2 + gg
                q = jnp.concatenate([qs[qp, :, wide_cols(g, hb, h)] for h in range(HB)], axis=0)
                k = jnp.concatenate([kv[slot + (pair, 0, gg)] for slot, _, _ in tiles], axis=1)
                got = jnp.dot(q, jnp.concatenate([k, k], axis=0), preferred_element_type=jnp.float32)
                out = []
                for n, (_, _, add) in enumerate(tiles):
                    sc = got[:, n * HEAD:(n + 1) * HEAD]
                    if isinstance(add, str):
                        sc = (sc.reshape(HB, TOK, TOK) + bias_s[...][None]).reshape(ROWS, TOK)
                    elif add is not None:
                        sc = sc + add
                    out.append(sc)
                return out

            def fold(unit, scs):
                gg, hb, qp, tiles = unit
                g = pair * 2 + gg
                span = pl.ds(hb * ROWS, ROWS)
                state = g * 2 + qp
                groups = {}
                for sc, (_, pen, _) in zip(scs, tiles):
                    groups.setdefault(id(pen), (pen, []))[1].append(sc)
                best = None
                for pen, members in groups.values():
                    top = members[0]
                    for one in members[1:]:
                        top = jnp.maximum(top, one)
                    top = jnp.max(top, axis=-1, keepdims=True)
                    top = top if pen is None else top - pen
                    best = top if best is None else jnp.maximum(best, top)
                best = jnp.broadcast_to(best, (ROWS, HEAD))
                if not first:
                    old = m_s[state, span, :]
                    best = jnp.maximum(old, best)
                    factor = jnp.exp2(old - best)
                shifts = {key: best if pen is None else best + pen for key, (pen, _) in groups.items()}
                ws = [jnp.exp2(sc - shifts[id(pen)]) for sc, (_, pen, _) in zip(scs, tiles)]
                w = jnp.concatenate([one.astype(jnp.bfloat16) for one in ws], axis=1)
                v = jnp.concatenate([kv[slot + (pair, 1, gg)] for slot, _, _ in tiles], axis=0)
                v = jnp.concatenate([v, jnp.ones_like(v)], axis=1)
                both = jnp.dot(w, v, preferred_element_type=jnp.float32)
                part, total = both[:, :HEAD], both[:, HEAD:]
                if not first:
                    total = l_s[state, span, :] * factor + total
                    part = acc_s[state, span, :] * factor + part
                if final:
                    res = (part / total).astype(jnp.bfloat16)
                    for h in range(HB):
                        obuf[qp, :, head_cols(g, hb, h)] = res[h * TOK:(h + 1) * TOK]
                else:
                    m_s[state, span, :] = best
                    l_s[state, span, :] = total
                    acc_s[state, span, :] = part

            ahead = scores(units[0])
            for n, unit in enumerate(units):
                scs = ahead
                if n + 1 < len(units):
                    ahead = scores(units[n + 1])
                fold(unit, scs)
                if final and unit[0] != (units + [(None,)])[n + 1][0]:
                    for copy in results(pair * 2 + unit[0]):
                        copy.start()

        def body(pair, carry):
            if any(e[0] == number * 2 + 1 for e in EVENTS + RELAY):
                pl.when(pair == 1)(lambda: events_at(number * 2 + 1))
            if everywhere:
                compute(pair)
            else:
                pl.when(not_first)(lambda: compute(pair))
            return carry

        job_now[0] = number
        if number == len(JOBS) - 1:
            drain(number - 2)
        events_at(number * 2)
        lax.fori_loop(0, 2, body, 0)

    def results(g):
        cols = pl.ds(pl.multiple_of(g * (8 * HEAD), HEAD), 8 * HEAD)
        ocols = pl.ds(pl.multiple_of((c * GROUPS + g) * (8 * HEAD), HEAD), 8 * HEAD)
        return (
            pltpu.make_async_copy(obuf.at[c, :, cols], o_ref.at[:, ocols], osem.at[0, g]),
            pltpu.make_async_remote_copy(
                src_ref=obuf.at[other, :, cols], dst_ref=o_ref.at[:, ocols],
                send_sem=osem.at[1, g], recv_sem=osem.at[2, g],
                device_id=dev_core, device_id_type=MESH),
        )

    locals_[2].wait()
    cores[0].wait_recv()

    def scale(h, carry):
        for qp in range(2):
            q = qbuf[qp, :, pl.ds(pl.multiple_of(h * HEAD, HEAD), HEAD)].astype(jnp.float32) * SCALE
            high = q.astype(jnp.bfloat16)
            low = (q - high.astype(jnp.float32)).astype(jnp.bfloat16)
            qs[qp, :, pl.ds(pl.multiple_of(h * (2 * HEAD), HEAD), HEAD)] = high
            qs[qp, :, pl.ds(pl.multiple_of(h * (2 * HEAD) + HEAD, HEAD), HEAD)] = low
        return carry

    lax.fori_loop(0, 8 * GROUPS, scale, 0, unroll=4)
    shared = [job[0][0] < 2 for job in JOBS]
    last_shared = max(n for n, one in enumerate(shared) if one)
    for number in range(last_shared + 1):
        run(number, JOBS[number], everywhere=shared[number])

    @pl.when(first_row)
    def _():
        def body(g, carry):
            for qp in range(2):
                for h in range(8):
                    span = pl.ds(h * TOK, TOK)
                    total = l_s[g * 2 + qp, span, :]
                    cols = pl.ds(pl.multiple_of((g * 8 + h) * HEAD, HEAD), HEAD)
                    obuf[qp, :, cols] = (acc_s[g * 2 + qp, span, :] / total).astype(jnp.bfloat16)
            for copy in results(g):
                copy.start()
            return carry

        lax.fori_loop(0, GROUPS, body, 0)

    for number in range(last_shared + 1, len(JOBS)):
        run(number, JOBS[number], final=number == len(JOBS) - 1)

    assert len(sends) <= 112
    drain(len(JOBS))
    for copy in cores:
        copy.wait_send()
    for g in range(GROUPS):
        mine, theirs = results(g)
        mine.wait()
        theirs.wait()


def local(queries, keys, values, lengths):
    dma = pltpu.SemaphoreType.DMA
    anywhere = pl.BlockSpec(memory_space=pl.ANY)
    queries, keys, values, lengths = (
        pltpu.with_memory_space_constraint(one, pltpu.HBM) for one in (queries, keys, values, lengths))
    return pl.pallas_call(
        kernel,
        out_shape=jax.ShapeDtypeStruct(queries.shape, jnp.bfloat16),
        in_specs=[anywhere] * 4,
        out_specs=anywhere,
        scratch_shapes=[
            pltpu.VMEM((5, 2, 4, 2, 2, 2, TOK, HEAD), jnp.bfloat16),
            pltpu.VMEM((2, 2, 2, TOK, HEAD), jnp.bfloat16),
            pltpu.VMEM((TOK, 2 * HALF), jnp.bfloat16),
            pltpu.VMEM((TOK, 2 * HALF), jnp.bfloat16),
            pltpu.VMEM((2, TOK, 8 * HALF), jnp.bfloat16),
            pltpu.VMEM((2, TOK, 16 * HALF), jnp.bfloat16),
            pltpu.VMEM((2, TOK, 8 * HALF), jnp.bfloat16),
            pltpu.VMEM((2 * GROUPS, 8 * TOK, HEAD), jnp.float32),
            pltpu.VMEM((2 * GROUPS, 8 * TOK, HEAD), jnp.float32),
            pltpu.VMEM((2 * GROUPS, 8 * TOK, HEAD), jnp.float32),
            pltpu.VMEM((TOK, TOK), jnp.float32),
            pltpu.SMEM((8,), jnp.int32),
            dma((5, 2, 4, 2)),
            dma((112,)),
            dma((4,)),
            dma((2,)),
            dma((2,)),
            dma((3, GROUPS)),
        ],
        compiler_params=pltpu.CompilerParams(
            collective_id=0, has_side_effects=True, vmem_limit_bytes=44 * 1024 * 1024),
        cost_estimate=pl.CostEstimate(flops=30_000_000_000, bytes_accessed=8_000_000, transcendentals=40_000_000),
    )(lengths, queries, keys, values)


def solution(mesh):
    split = P(("inst", "blk"), None)
    return jax.shard_map(local, mesh=mesh, in_specs=(split, split, split, P()), out_specs=split, check_vma=False)
```
